32 devices in a mesh: cable: 16 (over z, y, core), grid: 2 (over x).
Axes of the slice: x: 2, y: 2, z: 4, core: 2. Of those that a mesh axis runs over, the one named last changes fastest.
Arguments:
- green: bfloat16 [2, 4096, 4096], P(None, 'cable', 'grid'), may hold values from -6 to 6
- source_weight: float32 [4096], P('grid'), may hold values from 0.25 to 4
- observed: float32 [2, 2, 4096, 256], P(None, None, 'cable'), may hold values from -6 to 6
- amp_weight: float32 [2, 4096, 256], P(None, 'cable'), may hold values from 0.25 to 2
- pair_used: int32 [16, 2], P('cable'), may hold values 0 or 1
Outputs:
- adjoint: float32 [2, 4096, 4096], P(None, 'cable', 'grid')
- kernel: float32 [4096], P('grid')
The draws below stay inside these ranges and needn't reach their ends.
All inputs are finite; a program needn't handle non-finite values. No bound on the sum of `pair_used` on one device may be relied on, other than what follows from the above.
Results may differ from the reference program's by a relative error of at most 0.0037.
Values may be sent and summed in bfloat16 or wider, within the bound.
A program may use at most 64 MiB of HBM per device.

```python
import math
import jax
import jax.numpy as jnp
from jax import lax

NR = 256
NB = 16
RECV = 4096
GRID = 4096
N_CABLE = 16


def place_ends(drawn, own_key, smallest, top_value):
    longest = drawn.shape.index(max(drawn.shape))
    spots = []
    for shift in (0, 1):
        where = [jax.random.randint(jax.random.fold_in(own_key, axis), (), 0, length) for axis, length in enumerate(drawn.shape)]
        where[longest] = (where[longest] + shift) % drawn.shape[longest]
        spots.append(tuple(where))
    return drawn.at[spots[0]].set(smallest).at[spots[1]].set(top_value)


def levels(key, shape, split, low, largest):
    def one(position, parts):
        heights = jax.random.uniform(jax.random.fold_in(jax.random.fold_in(key, 6), position), (parts,), jnp.float32, low / len(split), largest / len(split))
        return jnp.repeat(jnp.exp(heights), shape[position] // parts).reshape((-1,) + (1,) * (len(shape) - position - 1))

    level = one(*split[0])
    for cut in split[1:]:
        level = level * one(*cut)
    return level


def scatter_about(stream_key, shape, deviation, most, shards=(), kind=jnp.bfloat16):
    entries = deviation * jax.random.normal(stream_key, shape, jnp.float32)
    if shards:
        entries = entries * levels(stream_key, shape, shards, -0.22, 0.18)
    return jnp.clip(entries, -most, most).astype(kind)


def setup_inputs(seed: int = 0) -> dict:
    seeds = jax.random.split(jax.random.key(seed), 6)
    return {
        "green": scatter_about(seeds[0], (2, RECV, GRID), 1.0, 6.0, ((1, 16), (2, 2))),
        "source_weight": jnp.clip(jnp.exp(math.log(4.0) - 2.7725887 * jax.random.uniform(seeds[1], (GRID,), jnp.float32) ** levels(seeds[1], (GRID,), ((0, 2),), -0.2, 0.2)), 0.25, 4.0),
        "observed": scatter_about(seeds[2], (2, 2, RECV, NR), 1.0, 6.0, ((2, 16),), jnp.float32),
        "amp_weight": jnp.clip(jnp.exp(math.log(2.0) - 2.0794415 * jax.random.uniform(seeds[3], (2, RECV, NR), jnp.float32) ** levels(seeds[3], (2, RECV, NR), ((1, 16),), -0.2, 0.2)), 0.25, 2.0),
        "pair_used": place_ends((jax.random.randint(seeds[4], (NB, 2), 0, 4) < 3).astype(jnp.int32), jax.random.fold_in(seeds[4], 1), 0, 1),
    }


def build_block(resid_real, resid_imag):
    upper_half = jnp.concatenate([resid_real, resid_imag], axis=1)
    lower_half = jnp.concatenate([-resid_imag, resid_real], axis=1)
    return jnp.concatenate([upper_half, lower_half], axis=0)

def reference(green, source_weight, observed, amp_weight, pair_used):
    block_count = N_CABLE
    row_count = NR
    col_count = green.shape[2]
    inv_norm = 1.0 / math.sqrt(col_count)
    kernel_scale = inv_norm / (2.0 * math.sqrt(2.0 * block_count))
    stacked = green.reshape(2, block_count, row_count, col_count).transpose(1, 0, 2, 3).reshape(block_count, 2 * row_count, col_count)

    def one_block(index, state_pair):
        fields, kernel = state_pair
        own_block = stacked[index]
        weighted = (own_block.astype(jnp.float32) * source_weight[None, :]).astype(jnp.bfloat16)
        for offset in range(2):
            places = offset + 1
            earlier = (index - places) % block_count
            partner = stacked[earlier]
            products = lax.dot_general(weighted, partner, (((1,), (1,)), ((), ())), preferred_element_type=jnp.float32)
            corr_real = inv_norm * (products[:row_count, :row_count] + products[row_count:, row_count:])
            corr_imag = inv_norm * (products[:row_count, row_count:] - products[row_count:, :row_count])
            observed_rows = lax.dynamic_slice_in_dim(observed[offset], (index * row_count).astype(jnp.int32), row_count, 1)
            weight_rows = lax.dynamic_slice_in_dim(amp_weight[offset], (index * row_count).astype(jnp.int32), row_count, 0)
            mask_value = pair_used[index, offset].astype(jnp.float32)
            resid_real = (mask_value * weight_rows * (corr_real - observed_rows[0])).astype(jnp.bfloat16)
            resid_imag = (mask_value * weight_rows * (corr_imag - observed_rows[1])).astype(jnp.bfloat16)
            resid_block = build_block(resid_real, resid_imag)
            later_term = jnp.dot(resid_block, partner, preferred_element_type=jnp.float32)
            early_term = lax.dot_general(resid_block, own_block, (((0,), (0,)), ((), ())), preferred_element_type=jnp.float32)
            kernel = kernel + lax.optimization_barrier(jnp.sum(own_block.astype(jnp.float32) * later_term, axis=0))
            fields = fields.at[index].add(later_term)
            fields = fields.at[earlier].add(early_term)
        return (fields, kernel)
    fields = jnp.zeros((block_count, 2 * row_count, col_count), jnp.float32)
    kernel = jnp.zeros((col_count,), jnp.float32)
    fields, kernel = lax.fori_loop(0, block_count, one_block, (fields, kernel))
    fields = inv_norm * source_weight[None, None, :] * fields
    adjoint = fields.reshape(block_count, 2, row_count, col_count).transpose(1, 0, 2, 3).reshape(2, block_count * row_count, col_count)
    return (adjoint, kernel * kernel_scale)
```

```python
import functools
import math

import jax
import jax.numpy as jnp
from jax import lax
from jax.experimental import pallas as pl
from jax.experimental.pallas import tpu as pltpu
from jax.sharding import PartitionSpec as P

MESH = pl.DeviceIdType.MESH
E1, E2, L1, L2 = 0, 1, 2, 3
CHUNKS = 8
HALVES = 2
LAG = 2


def body(cfg, green, weight, observed, amp, used, fields_out, kernel_out,
         near, weighted, corr_own, corr_in, resid_own, resid_in, later_mat, early_mat, acc, parts,
         mate_send, mate_recv, sib_send, sib_recv, far_send, far_recv, pass_send, pass_recv,
         corr_send, corr_recv, resid_send, resid_recv, part_send, part_recv, out_sem):
    n, ng, inv_norm, kernel_scale = cfg
    rows, cols = green.shape[1], green.shape[2]
    half_rows = rows // HALVES
    chunk_rows = rows // CHUNKS
    tile = min(512, cols)
    me = lax.axis_index("cable")
    gx = lax.axis_index("grid")
    core = lax.rem(me, 2)
    chip_odd = lax.rem(me // 2, 2)
    sign = 1 - 2 * chip_odd
    sibling = me + 1 - 2 * core
    mate = lax.rem(me + 2 * sign + n, n)
    onward = lax.rem(me + 4 * sign + n, n)
    mate_slot = L2 - 2 * chip_odd
    far_slot = E2 + 2 * chip_odd
    pass_from = L2 - 2 * core
    pass_to = L1 - 2 * core
    sib_to = E1 + 2 * core
    pass_is_mate = core == chip_odd

    barrier = pltpu.get_barrier_semaphore()

    def greet_cable(step, carry):
        pl.semaphore_signal(barrier, inc=1, device_id=(lax.rem(me + step, n), gx), device_id_type=MESH)
        return carry

    lax.fori_loop(1, n, greet_cable, 0)
    for step in range(1, ng):
        pl.semaphore_signal(barrier, inc=1, device_id=(me, lax.rem(gx + step, ng)), device_id_type=MESH)
    pl.semaphore_wait(barrier, n - 1 + ng - 1)

    def chunk(t):
        return pl.ds(t * chunk_rows, chunk_rows)

    def remote(src, dst, send, recv, cable, grid):
        return pltpu.make_async_remote_copy(
            src_ref=src, dst_ref=dst, send_sem=send, recv_sem=recv,
            device_id=(cable, grid), device_id_type=MESH)

    def to_mate(t):
        return remote(green.at[:, chunk(t), :], near.at[far_slot, :, chunk(t), :],
                      mate_send.at[t], mate_recv.at[t], mate, gx)

    def to_sib(h):
        spot = pl.ds(h * half_rows, half_rows)
        return remote(green.at[:, spot, :], near.at[sib_to, :, spot, :],
                      sib_send.at[h], sib_recv.at[h], sibling, gx)

    def to_far(t):
        return remote(near.at[mate_slot, :, chunk(t), :], near.at[far_slot, :, chunk(t), :],
                      far_send.at[t], far_recv.at[t], onward, gx)

    def to_pass(t):
        return remote(near.at[pass_from, :, chunk(t), :], near.at[pass_to, :, chunk(t), :],
                      pass_send.at[t], pass_recv.at[t], sibling, gx)

    def got_mate(t):
        remote(green.at[:, chunk(t), :], near.at[mate_slot, :, chunk(t), :],
               mate_send.at[t], mate_recv.at[t], mate, gx).wait_recv()

    def got_sib(h):
        spot = pl.ds(h * half_rows, half_rows)
        remote(green.at[:, spot, :], near.at[2 - sib_to, :, spot, :],
               sib_send.at[h], sib_recv.at[h], sibling, gx).wait_recv()

    def got_pass(t):
        remote(near.at[pass_from, :, chunk(t), :], near.at[2 - pass_to, :, chunk(t), :],
               pass_send.at[t], pass_recv.at[t], sibling, gx).wait_recv()

    def corr_copy(h, step):
        return remote(corr_own.at[h], corr_in.at[h, step - 1],
                      corr_send.at[h, step - 1], corr_recv.at[h, step - 1],
                      me, lax.rem(gx + step, ng))

    def resid_copy(h, o):
        return remote(resid_own.at[h, o], resid_in.at[h, o],
                      resid_send.at[h, o], resid_recv.at[h, o],
                      lax.rem(me - (o + 1) + n, n), gx)

    def correlate(h):
        spot = pl.ds(h * half_rows, half_rows)
        for o in range(2):
            other = near[o, :, spot, :].reshape(2 * half_rows, cols)
            prod = lax.dot_general(weighted[...], other, (((1,), (1,)), ((), ())),
                                   preferred_element_type=jnp.float32)
            corr_own[h, o, 0] = prod[:rows, :half_rows] + prod[rows:, half_rows:]
            corr_own[h, o, 1] = prod[:rows, half_rows:] - prod[rows:, :half_rows]
        for step in range(1, ng):
            corr_copy(h, step).start()

    def residual(h):
        for step in range(1, ng):
            corr_copy(h, step).wait()
        for o in range(2):
            mask = used[0, o].astype(jnp.float32) * amp[o, :, h * half_rows:(h + 1) * half_rows]
            pair = []
            for part in range(2):
                total = corr_own[h, o, part]
                for step in range(1, ng):
                    total = total + corr_in[h, step - 1, o, part]
                pair.append(mask * (inv_norm * total - observed[o, part, :, h * half_rows:(h + 1) * half_rows]))
            real, imag = pair
            resid_own[h, o, 0] = real.T.astype(jnp.bfloat16)
            resid_own[h, o, 1] = imag.T.astype(jnp.bfloat16)
            resid_copy(h, o).start()
            left = o * 2 * half_rows
            real16 = real.astype(jnp.bfloat16)
            imag16 = imag.astype(jnp.bfloat16)
            minus16 = (-imag).astype(jnp.bfloat16)
            later_mat[h, 0:rows, left:left + half_rows] = real16
            later_mat[h, 0:rows, left + half_rows:left + 2 * half_rows] = imag16
            later_mat[h, rows:2 * rows, left:left + half_rows] = minus16
            later_mat[h, rows:2 * rows, left + half_rows:left + 2 * half_rows] = real16

    def gather_early(h):
        for o in range(2):
            resid_copy(h, o).wait_recv()
            left = o * 2 * rows
            real = resid_in[h, o, 0]
            imag = resid_in[h, o, 1]
            early_mat[h, 0:half_rows, left:left + rows] = real
            early_mat[h, 0:half_rows, left + rows:left + 2 * rows] = -imag
            early_mat[h, half_rows:2 * half_rows, left:left + rows] = imag
            early_mat[h, half_rows:2 * half_rows, left + rows:left + 2 * rows] = real

    def later_terms(h):
        spot = pl.ds(h * half_rows, half_rows)

        def step(i, carry):
            at = pl.ds(pl.multiple_of(i * tile, tile), tile)
            other = near[E1:E2 + 1, :, spot, at].reshape(4 * half_rows, tile)
            term = jnp.dot(later_mat[h], other, preferred_element_type=jnp.float32).reshape(2, rows, tile)
            share = jnp.sum(green[:, :, at].astype(jnp.float32) * term, axis=(0, 1)).reshape(1, tile)
            if h == 0:
                acc[:, :, at] = term
                parts[me, :, at] = share
            else:
                acc[:, :, at] += term
                parts[me, :, at] += share
            return carry

        lax.fori_loop(0, cols // tile, step, 0)

    def early_terms(h):
        spot = pl.ds(h * half_rows, half_rows)

        def step(i, carry):
            at = pl.ds(pl.multiple_of(i * tile, tile), tile)
            other = near[L1:L2 + 1, :, :, at].reshape(4 * rows, tile)
            term = jnp.dot(early_mat[h], other, preferred_element_type=jnp.float32).reshape(2, half_rows, tile)
            acc[:, spot, at] += term
            return carry

        lax.fori_loop(0, cols // tile, step, 0)

    def scale_rows(h):
        spot = pl.ds(h * half_rows, half_rows)
        acc[:, spot, :] = acc[:, spot, :] * (inv_norm * weight[...]).reshape(1, 1, cols)

    def out_copy(h):
        spot = pl.ds(h * half_rows, half_rows)
        return pltpu.make_async_copy(acc.at[:, spot, :], fields_out.at[:, spot, :], out_sem.at[h])

    for t in range(CHUNKS):
        to_mate(t).start()
    for h in range(HALVES):
        to_sib(h).start()
    weighted[...] = (green[...].astype(jnp.float32) * weight[...].reshape(1, 1, cols)).astype(
        jnp.bfloat16).reshape(2 * rows, cols)
    for h in range(HALVES):
        got_sib(h)

    per_half = CHUNKS // HALVES

    def far_step(t):
        to_far(t).wait_recv()

        @pl.when(jnp.logical_not(pass_is_mate))
        def _():
            to_pass(t).start()

    for t in range(CHUNKS):
        got_mate(t)
        to_far(t).start()

        @pl.when(pass_is_mate)
        def _():
            to_pass(t).start()

        if t >= LAG:
            far_step(t - LAG)
        if t - LAG == per_half - 1:
            for u in range(per_half):
                got_pass(u)
            correlate(0)
    residual(0)
    for t in range(CHUNKS - LAG, CHUNKS):
        far_step(t)
    for u in range(per_half, CHUNKS):
        got_pass(u)
    correlate(1)
    later_terms(0)
    gather_early(0)
    early_terms(0)
    residual(1)
    later_terms(1)

    def part_copy(step):
        target = lax.rem(me + step, n)
        return remote(parts.at[me], parts.at[me], part_send.at[step], part_recv.at[me], target, gx)

    def part_start(step, carry):
        part_copy(step).start()
        return carry

    lax.fori_loop(1, n, part_start, 0)
    scale_rows(0)
    out_copy(0).start()
    gather_early(1)
    early_terms(1)
    scale_rows(1)
    out_copy(1).start()

    def part_wait(step, carry):
        source = lax.rem(me + step, n)
        remote(parts.at[me], parts.at[source], part_send.at[step], part_recv.at[source], source, gx).wait()
        return carry

    lax.fori_loop(1, n, part_wait, 0)

    def add_part(i, total):
        return total + parts[i]

    kernel_out[...] = kernel_scale * lax.fori_loop(1, n, add_part, parts[0])

    for t in range(CHUNKS):
        to_mate(t).wait_send()
        to_far(t).wait_send()
        to_pass(t).wait_send()
    for h in range(HALVES):
        to_sib(h).wait_send()
        for o in range(2):
            resid_copy(h, o).wait_send()
        out_copy(h).wait()


def shards(green, source_weight, observed, amp_weight, pair_used):
    rows, cols = green.shape[1], green.shape[2]
    n = lax.axis_size("cable")
    ng = lax.axis_size("grid")
    inv_norm = 1.0 / math.sqrt(cols * ng)
    kernel_scale = inv_norm / (2.0 * math.sqrt(2.0 * n))
    half = rows // HALVES
    peers = max(ng - 1, 1)
    f32, bf16 = jnp.float32, jnp.bfloat16
    dma = pltpu.SemaphoreType.DMA
    vmem = pl.BlockSpec(memory_space=pltpu.VMEM)
    adjoint, kernel = pl.pallas_call(
        functools.partial(body, (n, ng, inv_norm, kernel_scale)),
        out_shape=(jax.ShapeDtypeStruct((2, rows, cols), f32), jax.ShapeDtypeStruct((1, cols), f32)),
        in_specs=[vmem, vmem, vmem, vmem, pl.BlockSpec(memory_space=pltpu.SMEM)],
        out_specs=(pl.BlockSpec(memory_space=pl.ANY), vmem),
        scratch_shapes=[
            pltpu.VMEM((4, 2, rows, cols), bf16),
            pltpu.VMEM((2 * rows, cols), bf16),
            pltpu.VMEM((HALVES, 2, 2, rows, half), f32),
            pltpu.VMEM((HALVES, peers, 2, 2, rows, half), f32),
            pltpu.VMEM((HALVES, 2, 2, half, rows), bf16),
            pltpu.VMEM((HALVES, 2, 2, half, rows), bf16),
            pltpu.VMEM((HALVES, 2 * rows, 4 * half), bf16),
            pltpu.VMEM((HALVES, 2 * half, 4 * rows), bf16),
            pltpu.VMEM((2, rows, cols), f32),
            pltpu.VMEM((n, 1, cols), f32),
            dma((CHUNKS,)), dma((CHUNKS,)),
            dma((HALVES,)), dma((HALVES,)),
            dma((CHUNKS,)), dma((CHUNKS,)),
            dma((CHUNKS,)), dma((CHUNKS,)),
            dma((HALVES, peers)), dma((HALVES, peers)),
            dma((HALVES, 2)), dma((HALVES, 2)),
            dma((n,)), dma((n,)),
            dma((HALVES,)),
        ],
        compiler_params=pltpu.CompilerParams(
            collective_id=0, has_side_effects=True, vmem_limit_bytes=56 * 1024 * 1024),
        cost_estimate=pl.CostEstimate(flops=24 * rows * rows * cols * 2, bytes_accessed=20 * rows * cols, transcendentals=0),
    )(green, source_weight.reshape(1, cols), observed, amp_weight, pair_used)
    return (adjoint, kernel.reshape(cols))


def solution(mesh):
    in_specs = (
        P(None, "cable", "grid"),
        P("grid"),
        P(None, None, "cable", None),
        P(None, "cable", None),
        P("cable", None),
    )
    out_specs = (P(None, "cable", "grid"), P("grid"))
    return jax.shard_map(shards, mesh=mesh, in_specs=in_specs, out_specs=out_specs, check_vma=False)
```

```python
import functools
import math

import jax
import jax.numpy as jnp
from jax import lax
from jax.experimental import pallas as pl
from jax.experimental.pallas import tpu as pltpu
from jax.sharding import PartitionSpec as P

MESH = pl.DeviceIdType.MESH
E1, E2, L1, L2 = 0, 1, 2, 3
CHUNKS = 16
UNITS = 4
HALVES = 2
LAG = 3


def body(cfg, green, weight, observed, amp, used, acc, kernel_out,
         own, obs_in, amp_in, obs_t, amp_t, near, weighted, corr_own, corr_in, resid_own, resid_in, later_mat, early_mat, parts,
         mate_send, mate_recv, sib_send, sib_recv, far_send, far_recv, pass_send, pass_recv,
         corr_send, corr_recv, resid_send, resid_recv, part_send, part_recv, load_sem):
    n, ng, inv_norm, kernel_scale = cfg
    rows, cols = green.shape[1], green.shape[2]
    half_rows = rows // HALVES
    unit = rows // UNITS
    chunk_rows = rows // CHUNKS
    tile = min(512, cols)
    me = lax.axis_index("cable")
    gx = lax.axis_index("grid")
    core = lax.rem(me, 2)
    chip_odd = lax.rem(me // 2, 2)
    sign = 1 - 2 * chip_odd
    sibling = me + 1 - 2 * core
    mate = lax.rem(me + 2 * sign + n, n)
    onward = lax.rem(me + 4 * sign + n, n)
    mate_slot = L2 - 2 * chip_odd
    far_slot = E2 + 2 * chip_odd
    pass_from = L2 - 2 * core
    pass_to = L1 - 2 * core
    sib_to = E1 + 2 * core
    pass_is_mate = core == chip_odd

    barrier = pltpu.get_barrier_semaphore()

    def greet_cable(step, carry):
        pl.semaphore_signal(barrier, inc=1, device_id=(lax.rem(me + step, n), gx), device_id_type=MESH)
        return carry

    lax.fori_loop(1, n, greet_cable, 0)
    for step in range(1, ng):
        pl.semaphore_signal(barrier, inc=1, device_id=(me, lax.rem(gx + step, ng)), device_id_type=MESH)
    loads = [pltpu.make_async_copy(src, dst, load_sem.at[i])
             for i, (src, dst) in enumerate(((green, own), (observed, obs_in), (amp, amp_in)))]
    for copy in loads:
        copy.start()
    pl.semaphore_wait(barrier, n - 1 + ng - 1)

    def rows_of(u):
        return slice(u * unit, (u + 1) * unit)

    def chunk(t):
        return pl.ds(t * chunk_rows, chunk_rows)

    def remote(src, dst, send, recv, cable, grid):
        return pltpu.make_async_remote_copy(
            src_ref=src, dst_ref=dst, send_sem=send, recv_sem=recv,
            device_id=(cable, grid), device_id_type=MESH)

    def to_mate(t):
        return remote(green.at[:, chunk(t), :], near.at[far_slot, :, chunk(t), :],
                      mate_send.at[t], mate_recv.at[t], mate, gx)

    def to_sib(h):
        spot = pl.ds(h * half_rows, half_rows)
        return remote(green.at[:, spot, :], near.at[sib_to, :, spot, :],
                      sib_send.at[h], sib_recv.at[h], sibling, gx)

    def to_far(t):
        return remote(near.at[mate_slot, :, chunk(t), :], near.at[far_slot, :, chunk(t), :],
                      far_send.at[t], far_recv.at[t], onward, gx)

    def to_pass(t):
        return remote(near.at[pass_from, :, chunk(t), :], near.at[pass_to, :, chunk(t), :],
                      pass_send.at[t], pass_recv.at[t], sibling, gx)

    def got_mate(t):
        remote(green.at[:, chunk(t), :], near.at[mate_slot, :, chunk(t), :],
               mate_send.at[t], mate_recv.at[t], mate, gx).wait_recv()

    def got_sib(h):
        spot = pl.ds(h * half_rows, half_rows)
        remote(green.at[:, spot, :], near.at[2 - sib_to, :, spot, :],
               sib_send.at[h], sib_recv.at[h], sibling, gx).wait_recv()

    def got_pass(t):
        remote(near.at[pass_from, :, chunk(t), :], near.at[2 - pass_to, :, chunk(t), :],
               pass_send.at[t], pass_recv.at[t], sibling, gx).wait_recv()

    def corr_copy(u, step):
        return remote(corr_own.at[u], corr_in.at[u, step - 1],
                      corr_send.at[u, step - 1], corr_recv.at[u, step - 1],
                      me, lax.rem(gx + step, ng))

    def resid_copy(u, o):
        return remote(resid_own.at[u, o], resid_in.at[u, o],
                      resid_send.at[u, o], resid_recv.at[u, o],
                      lax.rem(me - (o + 1) + n, n), gx)

    def correlate(u):
        other = near[E1:E2 + 1, :, rows_of(u), :].reshape(4 * unit, cols)
        prod = lax.dot_general(other, weighted[...], (((1,), (1,)), ((), ())),
                               preferred_element_type=jnp.float32)
        for o in range(2):
            from_real = prod[2 * o * unit:(2 * o + 1) * unit]
            from_imag = prod[(2 * o + 1) * unit:(2 * o + 2) * unit]
            corr_own[u, o, 0] = from_real[:, :rows] + from_imag[:, rows:]
            corr_own[u, o, 1] = from_imag[:, :rows] - from_real[:, rows:]
        for step in range(1, ng):
            corr_copy(u, step).start()

    def fill(mat, top, left, real, imag):
        mat[top:top + unit, left:left + rows] = real
        mat[top:top + unit, left + rows:left + 2 * rows] = -imag
        mat[top + unit:top + 2 * unit, left:left + rows] = imag
        mat[top + unit:top + 2 * unit, left + rows:left + 2 * rows] = real

    def residual(u):
        for step in range(1, ng):
            corr_copy(u, step).wait()
        for o in range(2):
            pair = []
            for part in range(2):
                total = corr_own[u, o, part]
                for step in range(1, ng):
                    total = total + corr_in[u, step - 1, o, part]
                value = amp_t[o, rows_of(u), :] * (inv_norm * total - obs_t[o, part, rows_of(u), :])
                pair.append(value.astype(jnp.bfloat16))
            resid_own[u, o, 0] = pair[0]
            resid_own[u, o, 1] = pair[1]
            resid_copy(u, o).start()
            fill(later_mat, 4 * unit * u + 2 * unit * o, 0, pair[0], pair[1])

    def gather_early(u):
        for o in range(2):
            resid_copy(u, o).wait_recv()
            fill(early_mat, 2 * unit * u, 2 * rows * o, resid_in[u, o, 0], resid_in[u, o, 1])

    def later_terms(u):
        def step(i, carry):
            at = pl.ds(pl.multiple_of(i * tile, tile), tile)
            other = near[E1:E2 + 1, :, rows_of(u), at].reshape(4 * unit, tile)
            term = lax.dot_general(later_mat[4 * unit * u:4 * unit * (u + 1), :], other,
                                   (((0,), (0,)), ((), ())),
                                   preferred_element_type=jnp.float32).reshape(2, rows, tile)
            share = jnp.sum(own[:, :, at].astype(jnp.float32) * term, axis=(0, 1)).reshape(1, tile)
            if u == 0:
                acc[:, :, at] = term
                parts[me, :, at] = share
            else:
                acc[:, :, at] += term
                parts[me, :, at] += share
            return carry

        lax.fori_loop(0, cols // tile, step, 0)

    def early_terms(first, last):
        def step(i, carry):
            at = pl.ds(pl.multiple_of(i * tile, tile), tile)
            other = near[L1:L2 + 1, :, :, at].reshape(4 * rows, tile)
            term = jnp.dot(early_mat[2 * unit * first:2 * unit * last, :], other,
                           preferred_element_type=jnp.float32)
            for u in range(first, last):
                for part in range(2):
                    low = (2 * (u - first) + part) * unit
                    acc[part, rows_of(u), at] += term[low:low + unit]
            return carry

        lax.fori_loop(0, cols // tile, step, 0)

    for t in range(CHUNKS):
        to_mate(t).start()
    for h in range(HALVES):
        to_sib(h).start()
    for copy in loads:
        copy.wait()
    weighted[...] = (own[...].astype(jnp.float32) * weight[...].reshape(1, 1, cols)).astype(
        jnp.bfloat16).reshape(2 * rows, cols)
    for o in range(2):
        amp_t[o] = amp_in[o].T * used[0, o].astype(jnp.float32)
        for part in range(2):
            obs_t[o, part] = obs_in[o, part].T
    for h in range(HALVES):
        got_sib(h)

    per_unit = CHUNKS // UNITS

    def far_step(t):
        to_far(t).wait_recv()

        @pl.when(jnp.logical_not(pass_is_mate))
        def _():
            to_pass(t).start()

        if (t + 1) % per_unit == 0:
            u = t // per_unit
            for v in range(u * per_unit, (u + 1) * per_unit):
                got_pass(v)
            correlate(u)
            if u > 0:
                residual(u - 1)
                later_terms(u - 1)

    for t in range(CHUNKS):
        got_mate(t)
        to_far(t).start()

        @pl.when(pass_is_mate)
        def _():
            to_pass(t).start()

        if t >= LAG:
            far_step(t - LAG)
    for t in range(CHUNKS - LAG, CHUNKS):
        far_step(t)
    for u in range(UNITS - 1):
        gather_early(u)
    early_terms(0, UNITS - 1)
    residual(UNITS - 1)
    later_terms(UNITS - 1)

    def part_copy(step):
        target = lax.rem(me + step, n)
        return remote(parts.at[me], parts.at[me], part_send.at[step], part_recv.at[me], target, gx)

    def part_start(step, carry):
        part_copy(step).start()
        return carry

    lax.fori_loop(1, n, part_start, 0)
    gather_early(UNITS - 1)
    early_terms(UNITS - 1, UNITS)

    def part_wait(step, carry):
        source = lax.rem(me + step, n)
        remote(parts.at[me], parts.at[source], part_send.at[step], part_recv.at[source], source, gx).wait()
        return carry

    lax.fori_loop(1, n, part_wait, 0)

    def add_part(i, total):
        return total + parts[i]

    kernel_out[...] = kernel_scale * lax.fori_loop(1, n, add_part, parts[0])

    for t in range(CHUNKS):
        to_mate(t).wait_send()
        to_far(t).wait_send()
        to_pass(t).wait_send()
    for h in range(HALVES):
        to_sib(h).wait_send()
    for u in range(UNITS):
        for o in range(2):
            resid_copy(u, o).wait_send()


def shards(green, source_weight, observed, amp_weight, pair_used):
    rows, cols = green.shape[1], green.shape[2]
    n = lax.axis_size("cable")
    ng = lax.axis_size("grid")
    inv_norm = 1.0 / math.sqrt(cols * ng)
    kernel_scale = inv_norm / (2.0 * math.sqrt(2.0 * n))
    unit = rows // UNITS
    peers = max(ng - 1, 1)
    f32, bf16 = jnp.float32, jnp.bfloat16
    dma = pltpu.SemaphoreType.DMA
    vmem = pl.BlockSpec(memory_space=pltpu.VMEM)
    hbm = pl.BlockSpec(memory_space=pl.ANY)
    fields, kernel = pl.pallas_call(
        functools.partial(body, (n, ng, inv_norm, kernel_scale)),
        out_shape=(pltpu.VMEM((2, rows, cols), f32), jax.ShapeDtypeStruct((1, cols), f32)),
        in_specs=[hbm, vmem, hbm, hbm, pl.BlockSpec(memory_space=pltpu.SMEM)],
        out_specs=(vmem, vmem),
        scratch_shapes=[
            pltpu.VMEM((2, rows, cols), bf16),
            pltpu.VMEM((2, 2, rows, rows), f32),
            pltpu.VMEM((2, rows, rows), f32),
            pltpu.VMEM((2, 2, rows, rows), f32),
            pltpu.VMEM((2, rows, rows), f32),
            pltpu.VMEM((4, 2, rows, cols), bf16),
            pltpu.VMEM((2 * rows, cols), bf16),
            pltpu.VMEM((UNITS, 2, 2, unit, rows), f32),
            pltpu.VMEM((UNITS, peers, 2, 2, unit, rows), f32),
            pltpu.VMEM((UNITS, 2, 2, unit, rows), bf16),
            pltpu.VMEM((UNITS, 2, 2, unit, rows), bf16),
            pltpu.VMEM((4 * rows, 2 * rows), bf16),
            pltpu.VMEM((2 * rows, 4 * rows), bf16),
            pltpu.VMEM((n, 1, cols), f32),
            dma((CHUNKS,)), dma((CHUNKS,)),
            dma((HALVES,)), dma((HALVES,)),
            dma((CHUNKS,)), dma((CHUNKS,)),
            dma((CHUNKS,)), dma((CHUNKS,)),
            dma((UNITS, peers)), dma((UNITS, peers)),
            dma((UNITS, 2)), dma((UNITS, 2)),
            dma((n,)), dma((n,)),
            dma((3,)),
        ],
        compiler_params=pltpu.CompilerParams(
            collective_id=0, has_side_effects=True, vmem_limit_bytes=56 * 1024 * 1024),
        cost_estimate=pl.CostEstimate(flops=24 * rows * rows * cols * 2, bytes_accessed=20 * rows * cols, transcendentals=0),
    )(green, source_weight.reshape(1, cols), observed, amp_weight, pair_used)
    adjoint = (inv_norm * fields) * source_weight[None, None, :]
    return (adjoint, kernel.reshape(cols))


def solution(mesh):
    in_specs = (
        P(None, "cable", "grid"),
        P("grid"),
        P(None, None, "cable", None),
        P(None, "cable", None),
        P("cable", None),
    )
    out_specs = (P(None, "cable", "grid"), P("grid"))
    return jax.shard_map(shards, mesh=mesh, in_specs=in_specs, out_specs=out_specs, check_vma=False)
```

```python
import functools
import math

import jax
import jax.numpy as jnp
from jax import lax
from jax.experimental import pallas as pl
from jax.experimental.pallas import tpu as pltpu
from jax.sharding import PartitionSpec as P

MESH = pl.DeviceIdType.MESH
E1, E2, L1, L2 = 0, 1, 2, 3
CHUNKS = 16
SIZES = (7, 4, 3, 2)
UNITS = len(SIZES)
HALVES = 2
LAG = 3


def body(cfg, green, weight, observed, amp, used, acc, kernel_out, scale_out,
         own, obs_in, amp_in, obs_t, amp_t, near, weighted, corr_own, corr_in, resid_own, resid_in, later_mat, early_mat, parts,
         mate_send, mate_recv, sib_send, sib_recv, far_send, far_recv, pass_send, pass_recv,
         corr_send, corr_recv, resid_send, resid_recv, part_send, part_recv, load_sem):
    n, ng, inv_norm, kernel_scale = cfg
    rows, cols = green.shape[1], green.shape[2]
    half_rows = rows // HALVES
    sizes = [size * rows // sum(SIZES) for size in SIZES]
    begins = [sum(sizes[:u]) for u in range(UNITS)]
    chunk_rows = rows // CHUNKS
    tile = min(512, cols)
    me = lax.axis_index("cable")
    gx = lax.axis_index("grid")
    core = lax.rem(me, 2)
    chip_odd = lax.rem(me // 2, 2)
    sign = 1 - 2 * chip_odd
    sibling = me + 1 - 2 * core
    mate = lax.rem(me + 2 * sign + n, n)
    onward = lax.rem(me + 4 * sign + n, n)
    mate_slot = L2 - 2 * chip_odd
    far_slot = E2 + 2 * chip_odd
    pass_from = L2 - 2 * core
    pass_to = L1 - 2 * core
    sib_to = E1 + 2 * core
    pass_is_mate = core == chip_odd

    barrier = pltpu.get_barrier_semaphore()

    def greet_cable(step, carry):
        pl.semaphore_signal(barrier, inc=1, device_id=(lax.rem(me + step, n), gx), device_id_type=MESH)
        return carry

    lax.fori_loop(1, n, greet_cable, 0)
    for step in range(1, ng):
        pl.semaphore_signal(barrier, inc=1, device_id=(me, lax.rem(gx + step, ng)), device_id_type=MESH)
    loads = [pltpu.make_async_copy(src, dst, load_sem.at[i])
             for i, (src, dst) in enumerate(((green, own), (observed, obs_in), (amp, amp_in)))]
    for copy in loads:
        copy.start()
    pl.semaphore_wait(barrier, n - 1 + ng - 1)

    def rows_of(u):
        return slice(begins[u], begins[u] + sizes[u])

    def chunk(t):
        return pl.ds(t * chunk_rows, chunk_rows)

    def remote(src, dst, send, recv, cable, grid):
        return pltpu.make_async_remote_copy(
            src_ref=src, dst_ref=dst, send_sem=send, recv_sem=recv,
            device_id=(cable, grid), device_id_type=MESH)

    def to_mate(t):
        return remote(green.at[:, chunk(t), :], near.at[far_slot, :, chunk(t), :],
                      mate_send.at[t], mate_recv.at[t], mate, gx)

    def to_sib(h):
        spot = pl.ds(h * half_rows, half_rows)
        return remote(green.at[:, spot, :], near.at[sib_to, :, spot, :],
                      sib_send.at[h], sib_recv.at[h], sibling, gx)

    def to_far(t):
        return remote(near.at[mate_slot, :, chunk(t), :], near.at[far_slot, :, chunk(t), :],
                      far_send.at[t], far_recv.at[t], onward, gx)

    def to_pass(t):
        return remote(near.at[pass_from, :, chunk(t), :], near.at[pass_to, :, chunk(t), :],
                      pass_send.at[t], pass_recv.at[t], sibling, gx)

    def got_mate(t):
        remote(green.at[:, chunk(t), :], near.at[mate_slot, :, chunk(t), :],
               mate_send.at[t], mate_recv.at[t], mate, gx).wait_recv()

    def got_sib(h):
        spot = pl.ds(h * half_rows, half_rows)
        remote(green.at[:, spot, :], near.at[2 - sib_to, :, spot, :],
               sib_send.at[h], sib_recv.at[h], sibling, gx).wait_recv()

    def got_pass(t):
        remote(near.at[pass_from, :, chunk(t), :], near.at[2 - pass_to, :, chunk(t), :],
               pass_send.at[t], pass_recv.at[t], sibling, gx).wait_recv()

    def corr_copy(u, step):
        return remote(corr_own.at[:, :, rows_of(u), :], corr_in.at[step - 1, :, :, rows_of(u), :],
                      corr_send.at[u, step - 1], corr_recv.at[u, step - 1],
                      me, lax.rem(gx + step, ng))

    def resid_copy(u, o):
        return remote(resid_own.at[o, :, rows_of(u), :], resid_in.at[o, :, rows_of(u), :],
                      resid_send.at[u, o], resid_recv.at[u, o],
                      lax.rem(me - (o + 1) + n, n), gx)

    def correlate(u):
        unit = sizes[u]
        other = near[E1:E2 + 1, :, rows_of(u), :].reshape(4 * unit, cols)
        prod = lax.dot_general(other, weighted[...], (((1,), (1,)), ((), ())),
                               preferred_element_type=jnp.float32)
        for o in range(2):
            from_real = prod[2 * o * unit:(2 * o + 1) * unit]
            from_imag = prod[(2 * o + 1) * unit:(2 * o + 2) * unit]
            corr_own[o, 0, rows_of(u), :] = from_real[:, :rows] + from_imag[:, rows:]
            corr_own[o, 1, rows_of(u), :] = from_imag[:, :rows] - from_real[:, rows:]
        for step in range(1, ng):
            corr_copy(u, step).start()

    def fill(mat, unit, top, low, left, real, imag):
        mat[top:top + unit, left:left + rows] = real
        mat[top:top + unit, left + rows:left + 2 * rows] = -imag
        mat[low:low + unit, left:left + rows] = imag
        mat[low:low + unit, left + rows:left + 2 * rows] = real

    def residual(u):
        unit = sizes[u]
        for step in range(1, ng):
            corr_copy(u, step).wait()
        for o in range(2):
            pair = []
            for part in range(2):
                total = corr_own[o, part, rows_of(u), :]
                for step in range(1, ng):
                    total = total + corr_in[step - 1, o, part, rows_of(u), :]
                value = amp_t[o, rows_of(u), :] * (inv_norm * total - obs_t[o, part, rows_of(u), :])
                pair.append(value.astype(jnp.bfloat16))
            resid_own[o, 0, rows_of(u), :] = pair[0]
            resid_own[o, 1, rows_of(u), :] = pair[1]
            resid_copy(u, o).start()
            top = 4 * begins[u] + 2 * unit * o
            fill(later_mat, unit, top, top + unit, 0, pair[0], pair[1])

    def gather_early(u):
        for o in range(2):
            resid_copy(u, o).wait_recv()
            fill(early_mat, sizes[u], begins[u], rows + begins[u], 2 * rows * o,
                 resid_in[o, 0, rows_of(u), :], resid_in[o, 1, rows_of(u), :])

    def later_terms(u):
        unit = sizes[u]
        top = 4 * begins[u]
        def step(i, carry):
            at = pl.ds(pl.multiple_of(i * tile, tile), tile)
            other = near[E1:E2 + 1, :, rows_of(u), at].reshape(4 * unit, tile)
            term = lax.dot_general(later_mat[top:top + 4 * unit, :], other,
                                   (((0,), (0,)), ((), ())),
                                   preferred_element_type=jnp.float32).reshape(2, rows, tile)
            share = jnp.sum(own[:, :, at].astype(jnp.float32) * term, axis=(0, 1)).reshape(1, tile)
            if u == 0:
                acc[:, :, at] = term
                parts[me, :, at] = share
            else:
                acc[:, :, at] += term
                parts[me, :, at] += share
            return carry

        lax.fori_loop(0, cols // tile, step, 0)

    def early_terms():
        def step(i, carry):
            at = pl.ds(pl.multiple_of(i * tile, tile), tile)
            other = near[L1:L2 + 1, :, :, at].reshape(4 * rows, tile)
            acc[:, :, at] += jnp.dot(early_mat[...], other,
                                     preferred_element_type=jnp.float32).reshape(2, rows, tile)
            return carry

        lax.fori_loop(0, cols // tile, step, 0)

    for t in range(CHUNKS):
        to_mate(t).start()
    for h in range(HALVES):
        to_sib(h).start()
    scale_out[...] = inv_norm * weight[...]
    for copy in loads:
        copy.wait()
    weighted[...] = (own[...].astype(jnp.float32) * weight[...].reshape(1, 1, cols)).astype(
        jnp.bfloat16).reshape(2 * rows, cols)
    for o in range(2):
        amp_t[o] = amp_in[o].T * used[0, o].astype(jnp.float32)
        for part in range(2):
            obs_t[o, part] = obs_in[o, part].T
    for h in range(HALVES):
        got_sib(h)

    def far_step(t):
        to_far(t).wait_recv()

        @pl.when(jnp.logical_not(pass_is_mate))
        def _():
            to_pass(t).start()

        for u in range(UNITS):
            if (t + 1) * chunk_rows == begins[u] + sizes[u]:
                for v in range(begins[u] // chunk_rows, t + 1):
                    got_pass(v)
                correlate(u)
                if u > 0:
                    residual(u - 1)
                    later_terms(u - 1)

    for t in range(CHUNKS):
        got_mate(t)
        to_far(t).start()

        @pl.when(pass_is_mate)
        def _():
            to_pass(t).start()

        if t >= LAG:
            far_step(t - LAG)
    for t in range(CHUNKS - LAG, CHUNKS):
        far_step(t)
    for u in range(UNITS - 1):
        gather_early(u)
    residual(UNITS - 1)
    later_terms(UNITS - 1)

    def part_copy(step):
        target = lax.rem(me + step, n)
        return remote(parts.at[me], parts.at[me], part_send.at[step], part_recv.at[me], target, gx)

    def part_start(step, carry):
        part_copy(step).start()
        return carry

    lax.fori_loop(1, n, part_start, 0)
    gather_early(UNITS - 1)
    early_terms()

    def part_wait(step, carry):
        source = lax.rem(me + step, n)
        remote(parts.at[me], parts.at[source], part_send.at[step], part_recv.at[source], source, gx).wait()
        return carry

    lax.fori_loop(1, n, part_wait, 0)

    def add_part(i, total):
        return total + parts[i]

    kernel_out[...] = kernel_scale * lax.fori_loop(1, n, add_part, parts[0])

    for t in range(CHUNKS):
        to_mate(t).wait_send()
        to_far(t).wait_send()
        to_pass(t).wait_send()
    for h in range(HALVES):
        to_sib(h).wait_send()
    for u in range(UNITS):
        for o in range(2):
            resid_copy(u, o).wait_send()


def shards(green, source_weight, observed, amp_weight, pair_used):
    rows, cols = green.shape[1], green.shape[2]
    n = lax.axis_size("cable")
    ng = lax.axis_size("grid")
    inv_norm = 1.0 / math.sqrt(cols * ng)
    kernel_scale = inv_norm / (2.0 * math.sqrt(2.0 * n))
    peers = max(ng - 1, 1)
    f32, bf16 = jnp.float32, jnp.bfloat16
    dma = pltpu.SemaphoreType.DMA
    vmem = pl.BlockSpec(memory_space=pltpu.VMEM)
    hbm = pl.BlockSpec(memory_space=pl.ANY)
    fields, kernel, scale = pl.pallas_call(
        functools.partial(body, (n, ng, inv_norm, kernel_scale)),
        out_shape=(pltpu.VMEM((2, rows, cols), f32), jax.ShapeDtypeStruct((1, cols), f32), pltpu.VMEM((1, cols), f32)),
        in_specs=[hbm, vmem, hbm, hbm, pl.BlockSpec(memory_space=pltpu.SMEM)],
        out_specs=(vmem, vmem, vmem),
        scratch_shapes=[
            pltpu.VMEM((2, rows, cols), bf16),
            pltpu.VMEM((2, 2, rows, rows), f32),
            pltpu.VMEM((2, rows, rows), f32),
            pltpu.VMEM((2, 2, rows, rows), f32),
            pltpu.VMEM((2, rows, rows), f32),
            pltpu.VMEM((4, 2, rows, cols), bf16),
            pltpu.VMEM((2 * rows, cols), bf16),
            pltpu.VMEM((2, 2, rows, rows), f32),
            pltpu.VMEM((peers, 2, 2, rows, rows), f32),
            pltpu.VMEM((2, 2, rows, rows), bf16),
            pltpu.VMEM((2, 2, rows, rows), bf16),
            pltpu.VMEM((4 * rows, 2 * rows), bf16),
            pltpu.VMEM((2 * rows, 4 * rows), bf16),
            pltpu.VMEM((n, 1, cols), f32),
            dma((CHUNKS,)), dma((CHUNKS,)),
            dma((HALVES,)), dma((HALVES,)),
            dma((CHUNKS,)), dma((CHUNKS,)),
            dma((CHUNKS,)), dma((CHUNKS,)),
            dma((UNITS, peers)), dma((UNITS, peers)),
            dma((UNITS, 2)), dma((UNITS, 2)),
            dma((n,)), dma((n,)),
            dma((3,)),
        ],
        compiler_params=pltpu.CompilerParams(
            collective_id=0, has_side_effects=True, vmem_limit_bytes=56 * 1024 * 1024),
        cost_estimate=pl.CostEstimate(flops=24 * rows * rows * cols * 2, bytes_accessed=20 * rows * cols, transcendentals=0),
    )(green, source_weight.reshape(1, cols), observed, amp_weight, pair_used)
    adjoint = fields * scale[None, :, :]
    return (adjoint, kernel.reshape(cols))


def solution(mesh):
    in_specs = (
        P(None, "cable", "grid"),
        P("grid"),
        P(None, None, "cable", None),
        P(None, "cable", None),
        P("cable", None),
    )
    out_specs = (P(None, "cable", "grid"), P("grid"))
    return jax.shard_map(shards, mesh=mesh, in_specs=in_specs, out_specs=out_specs, check_vma=False)
```
